32 devices in a mesh: groups: 2 (over y), seq: 16 (over z, x, core).
Axes of the slice: x: 2, y: 2, z: 4, core: 2. Of those that a mesh axis runs over, the one named last changes fastest.
Arguments:
- queries: bfloat16 [8192, 4096], P(('groups', 'seq')), parts along dimension 0, may hold values from -6 to 6
- stretch_keys: bfloat16 [8192, 1024], P(('groups', 'seq')), parts along dimension 0, may hold values from -4 to 4
- prefill_values: bfloat16 [8192, 1024], P(('groups', 'seq')), parts along dimension 0, may hold values from -6 to 6
- earlier_keys: bfloat16 [16384, 1024], P(('groups', 'seq')), parts along dimension 0, may hold values from -6 to 6
- earlier_values: bfloat16 [16384, 1024], P(('groups', 'seq')), parts along dimension 0, may hold values from -6 to 6
- selected: int32 [16, 3], P('groups'), parts along dimension 0, may hold values from 0 to 15, all different within a row
Outputs:
- attended: bfloat16 [8192, 4096], P(('groups', 'seq')), parts along dimension 0
The draws below stay inside these ranges and needn't reach their ends.
There are 2 independent parts, one for each index of `groups`. The reference program is written for one: setup_inputs(seed, part) draws one part's arguments, and reference() takes and returns one part's arrays. A program takes and returns all parts, laid end to end along the dimension named above; each array names one. Nothing has to cross between parts.
Inputs may be any that keep to these rules, and one draw needn't show every extreme that they name: `selected`: each row names 3 different cache blocks, and every cache block is named by some row.
All inputs are finite; a program needn't handle non-finite values.
Results may differ from the reference program's by a relative error of at most 0.008.
Values may be sent and summed in bfloat16 or wider, within the bound.
A program may use at most 128 MiB of HBM per device.

```python
import jax
import jax.numpy as jnp
from jax import lax

QUERY_HEADS = 32
KEY_VALUE_HEADS = 8
HEAD_SIZE = 128
BLK = 512
TOPK = 3
QUERY_TOKENS = 4096
CACHE_POSITIONS = 8192
NQB = 8
NCB = 16


def draw_queries(key, part):
    key = jax.random.fold_in(key, 11)
    value_matrix = jnp.clip(jax.random.normal(key, (QUERY_TOKENS, QUERY_HEADS, HEAD_SIZE), jnp.float32), -4.0, 4.0)
    return value_matrix.reshape(QUERY_TOKENS, QUERY_HEADS * HEAD_SIZE).astype(jnp.bfloat16)


def draw_stretch_keys(key, part):
    key = jax.random.fold_in(key, 12)
    value_matrix = jnp.clip(jax.random.normal(key, (QUERY_TOKENS, KEY_VALUE_HEADS, HEAD_SIZE), jnp.float32), -4.0, 4.0)
    return value_matrix.reshape(QUERY_TOKENS, KEY_VALUE_HEADS * HEAD_SIZE).astype(jnp.bfloat16)


def level_of(rng, shape, split, low, high):
    factor_of, own = 1.0, jax.random.fold_in(rng, 6)
    for position, shards_of in split:
        steps = jnp.exp(jax.random.uniform(jax.random.fold_in(own, position), (shards_of,), jnp.float32, low / len(split), high / len(split)))
        factor_of = factor_of * jnp.repeat(steps, shape[position] // shards_of).reshape([-1 if axis == position else 1 for axis in range(len(shape))])
    return factor_of


def choose_distinct(rng, rows, count, top, lift):
    sequence = jax.random.permutation(jax.random.fold_in(rng, 1), count)
    favour = sequence
    for power in range(3):
        favour = favour * favour // count
    favour = favour * lift // count
    lots = jax.random.randint(jax.random.fold_in(rng, 2), (rows, count), 0, 4096) + favour
    sure = jax.random.permutation(jax.random.fold_in(rng, 3), rows)[jnp.arange(count) % rows]
    lots = jnp.where(jnp.arange(rows)[:, None] == sure[None, :], 1 << 14, lots)
    priority = lots * count + jnp.arange(count)
    return lax.top_k(priority.astype(jnp.int32), top)[1].astype(jnp.int32)


def bell_draw(rng, dims, width, bound, shards=(), held_as=jnp.bfloat16):
    gain = level_of(rng, dims, shards, -0.22, 0.18) if shards else 1.0
    entries = jax.random.normal(rng, dims, jnp.float32) * width * gain
    return jnp.minimum(jnp.maximum(entries, -bound), bound).astype(held_as)


def setup_inputs(seed: int = 0, part: int = 0) -> dict:
    keys = jax.random.split(jax.random.key(seed), 7)
    part_splits = jax.random.split(jax.random.fold_in(keys[6], part), 7)
    return {
        "queries": draw_queries(jax.random.fold_in(jax.random.fold_in(keys[6], part), 71), part),
        "stretch_keys": draw_stretch_keys(jax.random.fold_in(jax.random.fold_in(keys[6], part), 71), part),
        "prefill_values": bell_draw(part_splits[2], (QUERY_TOKENS, KEY_VALUE_HEADS * HEAD_SIZE), 1.0, 6.0, ((0, 16),)),
        "earlier_keys": bell_draw(part_splits[3], (CACHE_POSITIONS, KEY_VALUE_HEADS * HEAD_SIZE), 1.0, 6.0, ((0, 16),)),
        "earlier_values": bell_draw(part_splits[4], (CACHE_POSITIONS, KEY_VALUE_HEADS * HEAD_SIZE), 1.0, 6.0, ((0, 16),)),
        "selected": choose_distinct(part_splits[5], NQB, NCB, TOPK, 3072),
    }


def attend_block(rows_of_queries, rows_of_keys, rows_of_values, allowed):
    count_of_rows = rows_of_queries.shape[0]
    count_of_keys = rows_of_keys.shape[0]
    heads_of_queries = rows_of_queries.reshape(count_of_rows, KEY_VALUE_HEADS, QUERY_HEADS // KEY_VALUE_HEADS, HEAD_SIZE).astype(jnp.float32)
    heads_of_keys = rows_of_keys.reshape(count_of_keys, KEY_VALUE_HEADS, HEAD_SIZE).astype(jnp.float32)
    heads_of_values = rows_of_values.reshape(count_of_keys, KEY_VALUE_HEADS, HEAD_SIZE).astype(jnp.float32)
    scores = jnp.einsum("rhgd,khd->hgrk", heads_of_queries, heads_of_keys) * (HEAD_SIZE ** -0.5)
    scores = jnp.where(allowed[None, None], scores, -1e30)
    largest = jnp.max(scores, axis=-1, keepdims=True)
    expon = jnp.exp(scores - largest)
    weights = (expon / jnp.sum(expon, axis=-1, keepdims=True)).astype(jnp.bfloat16)
    result = jnp.einsum("hgrk,khd->rhgd", weights.astype(jnp.float32), heads_of_values)
    return result.reshape(count_of_rows, QUERY_HEADS * HEAD_SIZE).astype(jnp.bfloat16)


def reference(queries, stretch_keys, prefill_values, earlier_keys, earlier_values, selected):
    key_value_width = KEY_VALUE_HEADS * HEAD_SIZE
    cache_key_blocks = earlier_keys.reshape(NCB, BLK, key_value_width)
    cache_value_blocks = earlier_values.reshape(NCB, BLK, key_value_width)
    inside = jnp.arange(BLK, dtype=jnp.int32)
    causal = inside[None, :] <= inside[:, None]
    allowed = jnp.concatenate([jnp.ones((BLK, TOPK * BLK), dtype=bool), causal], axis=1)

    def one_block(block_id):
        start = (block_id * BLK).astype(jnp.int32)
        rows_of_queries = lax.dynamic_slice_in_dim(queries, start, BLK, 0)
        own_keys = lax.dynamic_slice_in_dim(stretch_keys, start, BLK, 0)
        own_values = lax.dynamic_slice_in_dim(prefill_values, start, BLK, 0)
        picks = selected[block_id]
        picked_keys = cache_key_blocks[picks].reshape(TOPK * BLK, key_value_width)
        picked_values = cache_value_blocks[picks].reshape(TOPK * BLK, key_value_width)
        rows_of_keys = jnp.concatenate([picked_keys, own_keys], axis=0)
        rows_of_values = jnp.concatenate([picked_values, own_values], axis=0)
        return attend_block(rows_of_queries, rows_of_keys, rows_of_values, allowed)

    outputs = lax.map(one_block, jnp.arange(NQB, dtype=jnp.int32))
    return outputs.reshape(QUERY_TOKENS, QUERY_HEADS * HEAD_SIZE)
```

```python
import functools

import jax
import jax.numpy as jnp
from jax import lax
from jax.experimental import pallas as pl
from jax.experimental.pallas import tpu as pltpu
from jax.sharding import PartitionSpec as P

QUERY_HEADS = 32
KEY_VALUE_HEADS = 8
HEAD_SIZE = 128
BLK = 512
TOPK = 3
CORES = 2
CHUNKS = KEY_VALUE_HEADS // CORES
SHARE = QUERY_HEADS // KEY_VALUE_HEADS
WIDE = SHARE * HEAD_SIZE
SCALE = HEAD_SIZE ** (-0.5) * 1.4426950408889634
MESH = pl.DeviceIdType.MESH


def attend_rows(q, keys, values, own_keys, own_values, first_row):
    contract = (((1,), (1,)), ((), ()))
    scores = lax.dot_general(q, keys, contract, preferred_element_type=jnp.float32)
    own = lax.dot_general(q, own_keys, contract, preferred_element_type=jnp.float32)
    row = lax.broadcasted_iota(jnp.int32, own.shape, 0) + first_row
    column = lax.broadcasted_iota(jnp.int32, own.shape, 1)
    own = jnp.where(column <= row, own, -1e30)
    largest = jnp.maximum(
        jnp.max(scores, axis=-1, keepdims=True), jnp.max(own, axis=-1, keepdims=True)
    ) * SCALE
    weights = jnp.exp2(scores * SCALE - largest).astype(jnp.bfloat16)
    own_weights = jnp.exp2(own * SCALE - largest).astype(jnp.bfloat16)

    def with_ones(block):
        return jnp.concatenate([block, jnp.ones_like(block)], axis=1)

    both = jnp.dot(weights, with_ones(values), preferred_element_type=jnp.float32)
    both += jnp.dot(own_weights, with_ones(own_values), preferred_element_type=jnp.float32)
    return (both[:, :HEAD_SIZE] / both[:, HEAD_SIZE:]).astype(jnp.bfloat16)


def kernel(
    members, holders,
    selected, queries, stretch_keys, stretch_values, cache_keys, cache_values,
    out,
    *scratch,
):
    held = scratch[:CHUNKS]
    staged, packed, kv, qs, outs = scratch[CHUNKS:CHUNKS + 5]
    (stage_sem, spread_send, spread_recv, fetch_send, fetch_recv,
     own_send, own_recv, q_send, q_recv, o_send, o_recv, o_local) = scratch[CHUNKS + 5:]

    me = lax.axis_index("seq")
    core = lax.rem(me, CORES)
    sibling = me + 1 - 2 * core
    base = (me // holders) * holders
    mine = lax.rem(me, holders)
    half = queries.shape[0]
    piece = BLK // holders
    my_rows = pl.ds(pl.multiple_of(core * half, half), half)
    other_rows = pl.ds(pl.multiple_of((1 - core) * half, half), half)

    for h in range(CHUNKS):
        for c in range(CORES):
            lanes = pl.ds((c * CHUNKS + h) * HEAD_SIZE, HEAD_SIZE)
            for n, source in enumerate((cache_keys, cache_values)):
                pltpu.make_async_copy(
                    source.at[:, lanes], staged.at[h, c, n], stage_sem.at[h]
                ).start()

    barrier = pltpu.get_barrier_semaphore()

    @pl.loop(1, members)
    def _(k):
        pl.semaphore_signal(
            barrier, inc=1, device_id={"seq": lax.rem(me + k, members)}, device_id_type=MESH
        )

    pl.semaphore_wait(barrier, members - 1)

    def spread(h):
        pltpu.make_async_copy(staged.at[h], staged.at[h], stage_sem.at[h]).wait()
        pltpu.make_async_copy(
            staged.at[h, :, :, pl.ds(pl.multiple_of(mine * piece, piece), piece), :],
            held[h].at[me], spread_recv.at[h],
        ).start()

        @pl.loop(1, members)
        def _(k):
            to = lax.rem(me + k, members)
            part = pl.multiple_of(lax.rem(to, holders) * piece, piece)
            pltpu.make_async_remote_copy(
                src_ref=staged.at[h, :, :, pl.ds(part, piece), :],
                dst_ref=held[h].at[me],
                send_sem=spread_send.at[h],
                recv_sem=spread_recv.at[h],
                device_id={"seq": to},
                device_id_type=MESH,
            ).start()

    spread(0)

    for h in range(CHUNKS):
        for here in (True, False):
            c = core if here else 1 - core
            q_lanes = pl.ds(pl.multiple_of((c * CHUNKS + h) * WIDE, WIDE), WIDE)
            kv_lanes = pl.ds(pl.multiple_of((c * CHUNKS + h) * HEAD_SIZE, HEAD_SIZE), HEAD_SIZE)
            for source, target, send, recv in (
                (queries.at[:, q_lanes], qs.at[h, my_rows, :], q_send, q_recv),
                (stretch_keys.at[:, kv_lanes], kv.at[h, TOPK, 0, my_rows, :], own_send, own_recv),
                (stretch_values.at[:, kv_lanes], kv.at[h, TOPK, 1, my_rows, :], own_send, own_recv),
            ):
                if here:
                    pltpu.make_async_copy(source, target, recv.at[h]).start()
                else:
                    pltpu.make_async_remote_copy(
                        src_ref=source, dst_ref=target, send_sem=send, recv_sem=recv.at[h],
                        device_id={"seq": sibling}, device_id_type=MESH,
                    ).start()

    for h in range(1, CHUNKS):
        spread(h)

    def fetch(h):
        pltpu.make_async_copy(held[h], held[h], spread_recv.at[h]).wait()
        land = kv.at[h, pl.ds(0, TOPK), :, pl.ds(pl.multiple_of(mine * piece, piece), piece), :]

        @pl.loop(0, holders)
        def _(k):
            i = lax.rem(mine + k, holders)
            to = base + i
            for t in range(TOPK):
                block = selected[to // CORES, t]
                packed[h, i, t] = held[h][block, lax.rem(to, CORES)]

            @pl.when(k == 0)
            def _():
                pltpu.make_async_copy(packed.at[h, i], land, fetch_recv.at[h]).start()

            @pl.when(k > 0)
            def _():
                pltpu.make_async_remote_copy(
                    src_ref=packed.at[h, i], dst_ref=land,
                    send_sem=fetch_send.at[h], recv_sem=fetch_recv.at[h],
                    device_id={"seq": to}, device_id_type=MESH,
                ).start()

    def attend(h):
        chosen = kv.at[h, pl.ds(0, TOPK)]
        pltpu.make_async_copy(chosen, chosen, fetch_recv.at[h]).wait()
        pltpu.make_async_copy(kv.at[h, TOPK], kv.at[h, TOPK], own_recv.at[h]).wait()
        pltpu.make_async_copy(qs.at[h], qs.at[h], q_recv.at[h]).wait()

        @pl.loop(0, SHARE)
        def _(g):
            lanes = pl.ds(pl.multiple_of(g * HEAD_SIZE, HEAD_SIZE), HEAD_SIZE)
            for r in range(CORES):
                rows = pl.ds(r * half, half)
                keys = kv[h, 0:TOPK, 0].reshape(TOPK * BLK, HEAD_SIZE)
                values = kv[h, 0:TOPK, 1].reshape(TOPK * BLK, HEAD_SIZE)
                seen = (r + 1) * half
                outs[h, rows, lanes] = attend_rows(
                    qs[h, rows, lanes], keys, values,
                    kv[h, TOPK, 0, 0:seen], kv[h, TOPK, 1, 0:seen], r * half,
                )

        lanes = pl.ds(pl.multiple_of((core * CHUNKS + h) * WIDE, WIDE), WIDE)
        pltpu.make_async_copy(outs.at[h, my_rows, :], out.at[:, lanes], o_local).start()
        pltpu.make_async_remote_copy(
            src_ref=outs.at[h, other_rows, :], dst_ref=out.at[:, lanes],
            send_sem=o_send, recv_sem=o_recv,
            device_id={"seq": sibling}, device_id_type=MESH,
        ).start()

    @pl.loop(0, CHUNKS + 1)
    def _(step):
        for h in range(CHUNKS):
            pl.when(step == h)(functools.partial(fetch, h))

        @pl.when(step > 0)
        def _():
            attend(step - 1)

    for h in range(CHUNKS):
        sent = held[h].at[pl.ds(0, members - 1)]
        pltpu.make_async_copy(sent, sent, spread_send.at[h]).wait()
        sent = packed.at[h, pl.ds(0, holders - 1)]
        pltpu.make_async_copy(sent, sent, fetch_send.at[h]).wait()
    sent = qs.at[pl.ds(0, CHUNKS // 2)]
    pltpu.make_async_copy(sent, sent, q_send).wait()
    sent = kv.at[pl.ds(0, CHUNKS // 2), TOPK]
    pltpu.make_async_copy(sent, sent, own_send).wait()
    wide = CHUNKS * WIDE
    kept = out.at[:, pl.ds(pl.multiple_of(core * wide, wide), wide)]
    given = out.at[:, pl.ds(pl.multiple_of((1 - core) * wide, wide), wide)]
    pltpu.make_async_copy(kept, kept, o_local).wait()
    pltpu.make_async_copy(kept, kept, o_send).wait()
    pltpu.make_async_copy(given, given, o_recv).wait()


def per_device(queries, stretch_keys, stretch_values, cache_keys, cache_values, selected):
    members = lax.axis_size("seq")
    half = queries.shape[0]
    assert half * CORES == BLK and cache_keys.shape[0] == BLK
    holders = min(members // 2, BLK // 16)
    piece = BLK // holders
    bf16 = jnp.bfloat16
    dma = pltpu.SemaphoreType.DMA
    anywhere = pl.BlockSpec(memory_space=pl.ANY)
    return pl.pallas_call(
        functools.partial(kernel, members, holders),
        out_shape=jax.ShapeDtypeStruct(queries.shape, bf16),
        in_specs=[pl.BlockSpec(memory_space=pltpu.SMEM)] + [anywhere] * 5,
        out_specs=anywhere,
        scratch_shapes=[
            pltpu.VMEM((members, CORES, 2, piece, HEAD_SIZE), bf16) for _ in range(CHUNKS)
        ] + [
            pltpu.VMEM((CHUNKS, CORES, 2, BLK, HEAD_SIZE), bf16),
            pltpu.VMEM((CHUNKS, holders, TOPK, 2, piece, HEAD_SIZE), bf16),
            pltpu.VMEM((CHUNKS, TOPK + 1, 2, BLK, HEAD_SIZE), bf16),
            pltpu.VMEM((CHUNKS, BLK, WIDE), bf16),
            pltpu.VMEM((CHUNKS, BLK, WIDE), bf16),
            dma((CHUNKS,)), dma((CHUNKS,)), dma((CHUNKS,)), dma((CHUNKS,)), dma((CHUNKS,)),
            dma, dma((CHUNKS,)), dma, dma((CHUNKS,)), dma, dma, dma,
        ],
        compiler_params=pltpu.CompilerParams(
            collective_id=0, has_side_effects=True, vmem_limit_bytes=56 * 1024 * 1024
        ),
        cost_estimate=pl.CostEstimate(
            flops=4 * half * QUERY_HEADS * HEAD_SIZE * (TOPK + 1) * BLK,
            bytes_accessed=16 << 20,
            transcendentals=half * QUERY_HEADS * (TOPK + 1) * BLK,
        ),
    )(selected, queries, stretch_keys, stretch_values, cache_keys, cache_values)


def solution(mesh):
    split = P(("groups", "seq"), None)
    return jax.shard_map(
        per_device,
        mesh=mesh,
        in_specs=(split, split, split, split, split, P("groups", None)),
        out_specs=split,
        check_vma=False,
    )
```

```python
import functools

import jax
import jax.numpy as jnp
from jax import lax
from jax.experimental import pallas as pl
from jax.experimental.pallas import tpu as pltpu
from jax.sharding import PartitionSpec as P

QUERY_HEADS = 32
KEY_VALUE_HEADS = 8
HEAD_SIZE = 128
BLK = 512
TOPK = 3
CORES = 2
CHUNKS = KEY_VALUE_HEADS // CORES
STAGES = 2 * CHUNKS
SHARE = QUERY_HEADS // KEY_VALUE_HEADS
WIDE = SHARE * HEAD_SIZE
SCALE = HEAD_SIZE ** (-0.5) * 1.4426950408889634
MESH = pl.DeviceIdType.MESH


CONTRACT = (((1,), (1,)), ((), ()))


def weighted(scores, largest, values):
    weights = jnp.exp2(scores * SCALE - largest * SCALE).astype(jnp.bfloat16)
    both = jnp.concatenate([values, jnp.ones_like(values)], axis=1)
    return jnp.dot(weights, both, preferred_element_type=jnp.float32)


def product(q, keys):
    return lax.dot_general(q, keys, CONTRACT, preferred_element_type=jnp.float32)


def attend_first(q, keys, values, own_keys, own_values, first_row):
    scores, own = product(q, keys), product(q, own_keys)
    row = lax.broadcasted_iota(jnp.int32, own.shape, 0) + first_row
    column = lax.broadcasted_iota(jnp.int32, own.shape, 1)
    own = jnp.where(column <= row, own, -1e30)
    largest = jnp.maximum(
        jnp.max(scores, axis=-1, keepdims=True), jnp.max(own, axis=-1, keepdims=True)
    )
    return weighted(scores, largest, values) + weighted(own, largest, own_values), largest


def attend_last(q, keys, values, both, before):
    scores = product(q, keys)
    largest = jnp.maximum(before, jnp.max(scores, axis=-1, keepdims=True))
    both = both * jnp.exp2((before - largest) * SCALE) + weighted(scores, largest, values)
    return (both[:, :HEAD_SIZE] / both[:, HEAD_SIZE:]).astype(jnp.bfloat16)


def kernel(
    members, holders, relayed,
    selected, queries, stretch_keys, stretch_values, cache_keys, cache_values,
    out,
    *scratch,
):
    held = scratch[:STAGES]
    staged, packed, kv, own, qs, outs, sums, tops = scratch[STAGES:STAGES + 8]
    (stage_sem, spread_send, spread_recv, near_recv, relay_send, fetch_send, fetch_recv,
     own_send, own_recv, q_send, q_recv, o_send, o_recv, o_local) = scratch[STAGES + 8:]

    me = lax.axis_index("seq")
    core = lax.rem(me, CORES)
    sibling = me + 1 - 2 * core
    mine = lax.rem(me, holders)
    if relayed:
        plane = me // holders
        upper = plane // 2
        set_size = 2 * holders
        base = upper * set_size
        inner = (1 + upper) * holders
        outer = 3 * upper * holders
        facing = (2 - upper) * holders
        away = lax.rem(plane + upper + 1, 2)
    else:
        set_size = holders
        base = (me // holders) * holders
    half = queries.shape[0]
    piece = BLK // (2 * holders)
    my_rows = pl.ds(pl.multiple_of(core * half, half), half)
    other_rows = pl.ds(pl.multiple_of((1 - core) * half, half), half)

    for h in range(CHUNKS):
        for c in range(CORES):
            lanes = pl.ds((c * CHUNKS + h) * HEAD_SIZE, HEAD_SIZE)
            for n, source in enumerate((cache_keys, cache_values)):
                pltpu.make_async_copy(
                    source.at[:, lanes], staged.at[h, c, n], stage_sem.at[h]
                ).start()

    barrier = pltpu.get_barrier_semaphore()

    @pl.loop(1, members)
    def _(k):
        pl.semaphore_signal(
            barrier, inc=1, device_id={"seq": lax.rem(me + k, members)}, device_id_type=MESH
        )

    pl.semaphore_wait(barrier, members - 1)

    def rows_of(s, holder):
        first = (s % 2) * (BLK // 2) + holder * piece
        return pl.ds(pl.multiple_of(first, piece), piece)

    def spread_near(s):
        h = s // 2

        @pl.loop(0, holders)
        def _(k):
            q = lax.rem(mine + k, holders)
            source = staged.at[h, :, :, rows_of(s, q), :]

            @pl.when(inner + q == me)
            def _():
                pltpu.make_async_copy(source, held[s].at[me], near_recv.at[s, away]).start()

            @pl.when(inner + q != me)
            def _():
                pltpu.make_async_remote_copy(
                    src_ref=source, dst_ref=held[s].at[me],
                    send_sem=spread_send.at[s], recv_sem=near_recv.at[s, away],
                    device_id={"seq": inner + q}, device_id_type=MESH,
                ).start()

    def relay(s):
        for n, first in enumerate((inner, outer)):
            blocks = held[s].at[pl.ds(first, holders)]
            pltpu.make_async_copy(blocks, blocks, near_recv.at[s, n]).wait()
            pltpu.make_async_remote_copy(
                src_ref=blocks, dst_ref=blocks,
                send_sem=relay_send.at[s], recv_sem=spread_recv.at[s],
                device_id={"seq": facing + mine}, device_id_type=MESH,
            ).start()

    def spread(s):
        h = s // 2
        if s % 2 == 0:
            pltpu.make_async_copy(staged.at[h], staged.at[h], stage_sem.at[h]).wait()
        if relayed:
            spread_near(s)
            return
        pltpu.make_async_copy(
            staged.at[h, :, :, rows_of(s, mine), :], held[s].at[me], spread_recv.at[s]
        ).start()

        @pl.loop(1, members)
        def _(k):
            to = lax.rem(me + k, members)
            pltpu.make_async_remote_copy(
                src_ref=staged.at[h, :, :, rows_of(s, lax.rem(to, holders)), :],
                dst_ref=held[s].at[me],
                send_sem=spread_send.at[s],
                recv_sem=spread_recv.at[s],
                device_id={"seq": to},
                device_id_type=MESH,
            ).start()

    spread(0)

    def holding(body, s):
        if relayed:
            pl.when(away == 0)(functools.partial(body, s))
        else:
            body(s)


    if relayed:
        spread(1)
        for s in range(2):
            holding(relay, s)
    for h in range(CHUNKS):
        for here in (True, False):
            c = core if here else 1 - core
            q_lanes = pl.ds(pl.multiple_of((c * CHUNKS + h) * WIDE, WIDE), WIDE)
            kv_lanes = pl.ds(pl.multiple_of((c * CHUNKS + h) * HEAD_SIZE, HEAD_SIZE), HEAD_SIZE)
            for source, target, send, recv in (
                (queries.at[:, q_lanes], qs.at[h, my_rows, :], q_send, q_recv),
                (stretch_keys.at[:, kv_lanes], own.at[h, 0, my_rows, :], own_send, own_recv),
                (stretch_values.at[:, kv_lanes], own.at[h, 1, my_rows, :], own_send, own_recv),
            ):
                if here:
                    pltpu.make_async_copy(source, target, recv.at[h]).start()
                else:
                    pltpu.make_async_remote_copy(
                        src_ref=source, dst_ref=target, send_sem=send, recv_sem=recv.at[h],
                        device_id={"seq": sibling}, device_id_type=MESH,
                    ).start()

    for s in range(2 if relayed else 1, STAGES if not relayed else 3):
        spread(s)

    def fetch(s):
        arrived = held[s].at[pl.ds(0, set_size)] if relayed else held[s]
        pltpu.make_async_copy(arrived, arrived, spread_recv.at[s]).wait()
        land = kv.at[s, :, :, pl.ds(pl.multiple_of(mine * piece, piece), piece), :]

        here = me - base

        @pl.loop(0, set_size)
        def _(k):
            i = lax.rem(here + k, set_size)
            to = base + i
            for t in range(TOPK):
                block = selected[t, to // CORES]
                packed[s, i, t] = held[s][block, lax.rem(to, CORES)]

            @pl.when(k == 0)
            def _():
                pltpu.make_async_copy(packed.at[s, i], land, fetch_recv.at[s]).start()

            @pl.when(k > 0)
            def _():
                pltpu.make_async_remote_copy(
                    src_ref=packed.at[s, i], dst_ref=land,
                    send_sem=fetch_send.at[s], recv_sem=fetch_recv.at[s],
                    device_id={"seq": to}, device_id_type=MESH,
                ).start()

    def picked(s, n):
        return kv[s, :, n].reshape(TOPK * BLK // 2, HEAD_SIZE)

    def tiles(body):
        @pl.loop(0, SHARE // 2)
        def _(pair):
            for u in range(2):
                g = pair * 2 + u
                lanes = pl.ds(pl.multiple_of(g * HEAD_SIZE, HEAD_SIZE), HEAD_SIZE)
                for r in range(CORES):
                    body(g, lanes, r, pl.ds(r * half, half))

    def first_part(h):
        s = 2 * h
        pltpu.make_async_copy(kv.at[s], kv.at[s], fetch_recv.at[s]).wait()
        pltpu.make_async_copy(own.at[h], own.at[h], own_recv.at[h]).wait()
        pltpu.make_async_copy(qs.at[h], qs.at[h], q_recv.at[h]).wait()

        def body(g, lanes, r, rows):
            seen = (r + 1) * half
            both, largest = attend_first(
                qs[h, rows, lanes], picked(s, 0), picked(s, 1),
                own[h, 0, 0:seen], own[h, 1, 0:seen], r * half,
            )
            sums[g, rows] = both
            tops[g, rows] = jnp.broadcast_to(largest, (half, HEAD_SIZE))

        tiles(body)

    def last_part(h):
        s = 2 * h + 1
        pltpu.make_async_copy(kv.at[s], kv.at[s], fetch_recv.at[s]).wait()

        def body(g, lanes, r, rows):
            outs[h, rows, lanes] = attend_last(
                qs[h, rows, lanes], picked(s, 0), picked(s, 1),
                sums[g, rows], tops[g, rows][:, :1],
            )

        tiles(body)

        lanes = pl.ds(pl.multiple_of((core * CHUNKS + h) * WIDE, WIDE), WIDE)
        pltpu.make_async_copy(outs.at[h, my_rows, :], out.at[:, lanes], o_local).start()
        pltpu.make_async_remote_copy(
            src_ref=outs.at[h, other_rows, :], dst_ref=out.at[:, lanes],
            send_sem=o_send, recv_sem=o_recv,
            device_id={"seq": sibling}, device_id_type=MESH,
        ).start()

    @pl.loop(0, STAGES + 1)
    def _(step):
        for s in range(STAGES):
            @pl.when(step == s)
            def _():
                if relayed and s + 2 < STAGES:
                    holding(relay, s + 2)
                if relayed and s + 3 < STAGES:
                    spread(s + 3)
                holding(fetch, s)

        @pl.when((step > 0) & (lax.rem(step, 2) == 1))
        def _():
            first_part((step - 1) // 2)

        @pl.when((step > 0) & (lax.rem(step, 2) == 0))
        def _():
            last_part((step - 1) // 2)

    def await_sent(count, s):
        sent = held[s].at[pl.ds(0, count)]
        pltpu.make_async_copy(sent, sent, spread_send.at[s]).wait()

    def await_held_sent(s):
        if relayed:
            await_sent(holders - 1, s)
            sent = held[s].at[pl.ds(0, set_size)]
            pltpu.make_async_copy(sent, sent, relay_send.at[s]).wait()
        sent = packed.at[s, pl.ds(0, set_size - 1)]
        pltpu.make_async_copy(sent, sent, fetch_send.at[s]).wait()

    for s in range(STAGES):
        if relayed:
            pl.when(away == 1)(functools.partial(await_sent, holders, s))
        else:
            await_sent(members - 1, s)
        holding(await_held_sent, s)
    sent = qs.at[pl.ds(0, CHUNKS // 2)]
    pltpu.make_async_copy(sent, sent, q_send).wait()
    sent = own.at[pl.ds(0, CHUNKS // 2)]
    pltpu.make_async_copy(sent, sent, own_send).wait()
    wide = CHUNKS * WIDE
    kept = out.at[:, pl.ds(pl.multiple_of(core * wide, wide), wide)]
    given = out.at[:, pl.ds(pl.multiple_of((1 - core) * wide, wide), wide)]
    pltpu.make_async_copy(kept, kept, o_local).wait()
    pltpu.make_async_copy(kept, kept, o_send).wait()
    pltpu.make_async_copy(given, given, o_recv).wait()


def per_device(queries, stretch_keys, stretch_values, cache_keys, cache_values, selected):
    members = lax.axis_size("seq")
    half = queries.shape[0]
    assert half * CORES == BLK and cache_keys.shape[0] == BLK
    relayed = members == 16
    holders = members // 4 if relayed else min(members // 2, BLK // 32)
    set_size = 2 * holders if relayed else holders
    piece = BLK // (2 * holders)
    bf16 = jnp.bfloat16
    dma = pltpu.SemaphoreType.DMA
    anywhere = pl.BlockSpec(memory_space=pl.ANY)
    return pl.pallas_call(
        functools.partial(kernel, members, holders, relayed),
        out_shape=jax.ShapeDtypeStruct(queries.shape, bf16),
        in_specs=[pl.BlockSpec(memory_space=pltpu.SMEM)] + [anywhere] * 5,
        out_specs=anywhere,
        scratch_shapes=[
            pltpu.VMEM((members, CORES, 2, piece, HEAD_SIZE), bf16) for _ in range(STAGES)
        ] + [
            pltpu.VMEM((CHUNKS, CORES, 2, BLK, HEAD_SIZE), bf16),
            pltpu.VMEM((STAGES, set_size, TOPK, 2, piece, HEAD_SIZE), bf16),
            pltpu.VMEM((STAGES, TOPK, 2, BLK // 2, HEAD_SIZE), bf16),
            pltpu.VMEM((CHUNKS, 2, BLK, HEAD_SIZE), bf16),
            pltpu.VMEM((CHUNKS, BLK, WIDE), bf16),
            pltpu.VMEM((CHUNKS, BLK, WIDE), bf16),
            pltpu.VMEM((SHARE, BLK, 2 * HEAD_SIZE), jnp.float32),
            pltpu.VMEM((SHARE, BLK, HEAD_SIZE), jnp.float32),
            dma((CHUNKS,)), dma((STAGES,)), dma((STAGES,)), dma((STAGES, 2)), dma((STAGES,)),
            dma((STAGES,)), dma((STAGES,)),
            dma, dma((CHUNKS,)), dma, dma((CHUNKS,)), dma, dma, dma,
        ],
        compiler_params=pltpu.CompilerParams(
            collective_id=0, has_side_effects=True, vmem_limit_bytes=56 * 1024 * 1024
        ),
        cost_estimate=pl.CostEstimate(
            flops=4 * half * QUERY_HEADS * HEAD_SIZE * (TOPK + 1) * BLK,
            bytes_accessed=16 << 20,
            transcendentals=half * QUERY_HEADS * (TOPK + 1) * BLK,
        ),
    )(selected.T, queries, stretch_keys, stretch_values, cache_keys, cache_values)


def solution(mesh):
    split = P(("groups", "seq"), None)
    return jax.shard_map(
        per_device,
        mesh=mesh,
        in_specs=(split, split, split, split, split, P("groups", None)),
        out_specs=split,
        check_vma=False,
    )
```

```python
import functools

import jax
import jax.numpy as jnp
from jax import lax
from jax.experimental import pallas as pl
from jax.experimental.pallas import tpu as pltpu
from jax.sharding import PartitionSpec as P

QUERY_HEADS = 32
KEY_VALUE_HEADS = 8
HEAD_SIZE = 128
BLK = 512
TOPK = 3
CORES = 2
CHUNKS = KEY_VALUE_HEADS // CORES
SHARE = QUERY_HEADS // KEY_VALUE_HEADS
WIDE = SHARE * HEAD_SIZE
SCALE = HEAD_SIZE ** (-0.5) * 1.4426950408889634
MESH = pl.DeviceIdType.MESH


CONTRACT = (((1,), (1,)), ((), ()))


def weighted(scores, largest, values):
    weights = jnp.exp2(scores * SCALE - largest * SCALE).astype(jnp.bfloat16)
    both = jnp.concatenate([values, jnp.ones_like(values)], axis=1)
    return jnp.dot(weights, both, preferred_element_type=jnp.float32)


def product(q, keys):
    return lax.dot_general(q, keys, CONTRACT, preferred_element_type=jnp.float32)


def attend_first(q, keys, values, own_keys, own_values, first_row):
    scores, own = product(q, keys), product(q, own_keys)
    row = lax.broadcasted_iota(jnp.int32, own.shape, 0) + first_row
    column = lax.broadcasted_iota(jnp.int32, own.shape, 1)
    own = jnp.where(column <= row, own, -1e30)
    largest = jnp.maximum(
        jnp.max(scores, axis=-1, keepdims=True), jnp.max(own, axis=-1, keepdims=True)
    )
    return weighted(scores, largest, values) + weighted(own, largest, own_values), largest


def attend_later(q, keys, values, both, before):
    scores = product(q, keys)
    largest = jnp.maximum(before, jnp.max(scores, axis=-1, keepdims=True))
    both = both * jnp.exp2((before - largest) * SCALE) + weighted(scores, largest, values)
    return both, largest


def kernel(
    members, holders, relayed, parts,
    selected, queries, stretch_keys, stretch_values, cache_keys, cache_values,
    out,
    *scratch,
):
    stages = CHUNKS * len(parts)
    held = scratch[:stages]
    staged, packed, kv, own, qs, outs, sums, tops = scratch[stages:stages + 8]
    (stage_sem, spread_send, spread_recv, near_recv, relay_send, fetch_send, fetch_recv,
     own_send, own_recv, q_send, q_recv, o_send, o_recv, o_local) = scratch[stages + 8:]

    me = lax.axis_index("seq")
    core = lax.rem(me, CORES)
    sibling = me + 1 - 2 * core
    mine = lax.rem(me, holders)
    if relayed:
        plane = me // holders
        upper = plane // 2
        set_size = 2 * holders
        base = upper * set_size
        inner = (1 + upper) * holders
        outer = 3 * upper * holders
        facing = (2 - upper) * holders
        away = lax.rem(plane + upper + 1, 2)
    else:
        set_size = holders
        base = (me // holders) * holders
    half = queries.shape[0]
    my_rows = pl.ds(pl.multiple_of(core * half, half), half)
    other_rows = pl.ds(pl.multiple_of((1 - core) * half, half), half)

    for h in range(CHUNKS):
        for c in range(CORES):
            lanes = pl.ds((c * CHUNKS + h) * HEAD_SIZE, HEAD_SIZE)
            for n, source in enumerate((cache_keys, cache_values)):
                pltpu.make_async_copy(
                    source.at[:, lanes], staged.at[h, c, n], stage_sem.at[h]
                ).start()

    barrier = pltpu.get_barrier_semaphore()

    @pl.loop(1, members)
    def _(k):
        pl.semaphore_signal(
            barrier, inc=1, device_id={"seq": lax.rem(me + k, members)}, device_id_type=MESH
        )

    pl.semaphore_wait(barrier, members - 1)

    def rows_of(s, holder):
        n = s % len(parts)
        first = sum(parts[:n]) * holders + holder * parts[n]
        return pl.ds(pl.multiple_of(first, 16), parts[n])

    def spread_near(s):
        h = s // len(parts)

        @pl.loop(0, holders)
        def _(k):
            q = lax.rem(mine + k, holders)
            source = staged.at[h, :, :, rows_of(s, q), :]

            @pl.when(inner + q == me)
            def _():
                pltpu.make_async_copy(source, held[s].at[me], near_recv.at[s, away]).start()

            @pl.when(inner + q != me)
            def _():
                pltpu.make_async_remote_copy(
                    src_ref=source, dst_ref=held[s].at[me],
                    send_sem=spread_send.at[s], recv_sem=near_recv.at[s, away],
                    device_id={"seq": inner + q}, device_id_type=MESH,
                ).start()

    def relay(s):
        for n, first in enumerate((inner, outer)):
            blocks = held[s].at[pl.ds(first, holders)]
            pltpu.make_async_copy(blocks, blocks, near_recv.at[s, n]).wait()
            pltpu.make_async_remote_copy(
                src_ref=blocks, dst_ref=blocks,
                send_sem=relay_send.at[s], recv_sem=spread_recv.at[s],
                device_id={"seq": facing + mine}, device_id_type=MESH,
            ).start()

    def spread(s):
        h = s // len(parts)
        if s % len(parts) == 0:
            pltpu.make_async_copy(staged.at[h], staged.at[h], stage_sem.at[h]).wait()
        if relayed:
            spread_near(s)
            return
        pltpu.make_async_copy(
            staged.at[h, :, :, rows_of(s, mine), :], held[s].at[me], spread_recv.at[s]
        ).start()

        @pl.loop(1, members)
        def _(k):
            to = lax.rem(me + k, members)
            pltpu.make_async_remote_copy(
                src_ref=staged.at[h, :, :, rows_of(s, lax.rem(to, holders)), :],
                dst_ref=held[s].at[me],
                send_sem=spread_send.at[s],
                recv_sem=spread_recv.at[s],
                device_id={"seq": to},
                device_id_type=MESH,
            ).start()

    spread(0)

    def holding(body, s):
        if relayed:
            pl.when(away == 0)(functools.partial(body, s))
        else:
            body(s)


    if relayed:
        spread(1)
        for s in range(2):
            holding(relay, s)
    for h in range(CHUNKS):
        for here in (True, False):
            c = core if here else 1 - core
            q_lanes = pl.ds(pl.multiple_of((c * CHUNKS + h) * WIDE, WIDE), WIDE)
            kv_lanes = pl.ds(pl.multiple_of((c * CHUNKS + h) * HEAD_SIZE, HEAD_SIZE), HEAD_SIZE)
            for source, target, send, recv in (
                (queries.at[:, q_lanes], qs.at[h, my_rows, :], q_send, q_recv),
                (stretch_keys.at[:, kv_lanes], own.at[h, 0, my_rows, :], own_send, own_recv),
                (stretch_values.at[:, kv_lanes], own.at[h, 1, my_rows, :], own_send, own_recv),
            ):
                if here:
                    pltpu.make_async_copy(source, target, recv.at[h]).start()
                else:
                    pltpu.make_async_remote_copy(
                        src_ref=source, dst_ref=target, send_sem=send, recv_sem=recv.at[h],
                        device_id={"seq": sibling}, device_id_type=MESH,
                    ).start()

    for s in range(2 if relayed else 1, stages if not relayed else 3):
        spread(s)

    def fetch(s):
        arrived = held[s].at[pl.ds(0, set_size)] if relayed else held[s]
        pltpu.make_async_copy(arrived, arrived, spread_recv.at[s]).wait()
        piece = parts[s % len(parts)]
        land = kv.at[s, :, :, pl.ds(pl.multiple_of(mine * piece, piece), piece), :]
        kept = pl.ds(0, piece)

        here = me - base

        @pl.loop(0, set_size)
        def _(k):
            i = lax.rem(here + k, set_size)
            to = base + i
            for t in range(TOPK):
                block = selected[t, to // CORES]
                packed[s, i, t, :, 0:piece] = held[s][block, lax.rem(to, CORES)]

            @pl.when(k == 0)
            def _():
                pltpu.make_async_copy(packed.at[s, i, :, :, kept], land, fetch_recv.at[s]).start()

            @pl.when(k > 0)
            def _():
                pltpu.make_async_remote_copy(
                    src_ref=packed.at[s, i, :, :, kept], dst_ref=land,
                    send_sem=fetch_send.at[s], recv_sem=fetch_recv.at[s],
                    device_id={"seq": to}, device_id_type=MESH,
                ).start()

    def picked(s, n, n_part):
        rows = parts[n_part] * holders
        return kv[s, :, n, 0:rows].reshape(TOPK * rows, HEAD_SIZE)

    def await_picked(s, n_part):
        arrived = kv.at[s, :, :, pl.ds(0, parts[n_part] * holders)]
        pltpu.make_async_copy(arrived, arrived, fetch_recv.at[s]).wait()

    def tiles(body):
        @pl.loop(0, SHARE // 2)
        def _(pair):
            for u in range(2):
                g = pair * 2 + u
                lanes = pl.ds(pl.multiple_of(g * HEAD_SIZE, HEAD_SIZE), HEAD_SIZE)
                for r in range(CORES):
                    body(g, lanes, r, pl.ds(r * half, half))

    def first_part(h):
        s = len(parts) * h
        await_picked(s, 0)
        pltpu.make_async_copy(own.at[h], own.at[h], own_recv.at[h]).wait()
        pltpu.make_async_copy(qs.at[h], qs.at[h], q_recv.at[h]).wait()

        def body(g, lanes, r, rows):
            seen = (r + 1) * half
            both, largest = attend_first(
                qs[h, rows, lanes], picked(s, 0, 0), picked(s, 1, 0),
                own[h, 0, 0:seen], own[h, 1, 0:seen], r * half,
            )
            sums[g, rows] = both
            tops[g, rows] = jnp.broadcast_to(largest, (half, HEAD_SIZE))

        tiles(body)

    def later_part(h, n_part):
        s = len(parts) * h + n_part
        await_picked(s, n_part)

        def body(g, lanes, r, rows):
            both, largest = attend_later(
                qs[h, rows, lanes], picked(s, 0, n_part), picked(s, 1, n_part),
                sums[g, rows], tops[g, rows][:, :1],
            )
            if n_part < len(parts) - 1:
                sums[g, rows] = both
                tops[g, rows] = jnp.broadcast_to(largest, (half, HEAD_SIZE))
            else:
                done = both[:, :HEAD_SIZE] / both[:, HEAD_SIZE:]
                outs[h, rows, lanes] = done.astype(jnp.bfloat16)

        tiles(body)
        if n_part == len(parts) - 1:
            give_back(h)

    def give_back(h):
        lanes = pl.ds(pl.multiple_of((core * CHUNKS + h) * WIDE, WIDE), WIDE)
        pltpu.make_async_copy(outs.at[h, my_rows, :], out.at[:, lanes], o_local).start()
        pltpu.make_async_remote_copy(
            src_ref=outs.at[h, other_rows, :], dst_ref=out.at[:, lanes],
            send_sem=o_send, recv_sem=o_recv,
            device_id={"seq": sibling}, device_id_type=MESH,
        ).start()

    @pl.loop(0, stages + 1)
    def _(step):
        for s in range(stages):
            @pl.when(step == s)
            def _():
                if relayed and s + 2 < stages:
                    holding(relay, s + 2)
                if relayed and s + 3 < stages:
                    spread(s + 3)
                holding(fetch, s)

        before = step - 1

        @pl.when((step > 0) & (lax.rem(before, len(parts)) == 0))
        def _():
            first_part(before // len(parts))

        for n_part in range(1, len(parts)):
            @pl.when((step > 0) & (lax.rem(before, len(parts)) == n_part))
            def _():
                later_part(before // len(parts), n_part)

    def await_sent(count, s):
        sent = held[s].at[pl.ds(0, count)]
        pltpu.make_async_copy(sent, sent, spread_send.at[s]).wait()

    def await_held_sent(s):
        if relayed:
            await_sent(holders - 1, s)
            sent = held[s].at[pl.ds(0, set_size)]
            pltpu.make_async_copy(sent, sent, relay_send.at[s]).wait()
        sent = packed.at[s, pl.ds(0, set_size - 1), :, :, pl.ds(0, parts[s % len(parts)])]
        pltpu.make_async_copy(sent, sent, fetch_send.at[s]).wait()

    for s in range(stages):
        if relayed:
            pl.when(away == 1)(functools.partial(await_sent, holders, s))
        else:
            await_sent(members - 1, s)
        holding(await_held_sent, s)
    sent = qs.at[pl.ds(0, CHUNKS // 2)]
    pltpu.make_async_copy(sent, sent, q_send).wait()
    sent = own.at[pl.ds(0, CHUNKS // 2)]
    pltpu.make_async_copy(sent, sent, own_send).wait()
    wide = CHUNKS * WIDE
    kept = out.at[:, pl.ds(pl.multiple_of(core * wide, wide), wide)]
    given = out.at[:, pl.ds(pl.multiple_of((1 - core) * wide, wide), wide)]
    pltpu.make_async_copy(kept, kept, o_local).wait()
    pltpu.make_async_copy(kept, kept, o_send).wait()
    pltpu.make_async_copy(given, given, o_recv).wait()


def per_device(queries, stretch_keys, stretch_values, cache_keys, cache_values, selected):
    members = lax.axis_size("seq")
    half = queries.shape[0]
    assert half * CORES == BLK and cache_keys.shape[0] == BLK
    relayed = members == 16
    holders = members // 4 if relayed else min(members // 2, BLK // 32)
    set_size = 2 * holders if relayed else holders
    parts = (BLK // 8, BLK // 16, BLK // 16) if relayed else (BLK // (2 * holders),) * 2
    stages = CHUNKS * len(parts)
    bf16 = jnp.bfloat16
    dma = pltpu.SemaphoreType.DMA
    anywhere = pl.BlockSpec(memory_space=pl.ANY)
    return pl.pallas_call(
        functools.partial(kernel, members, holders, relayed, parts),
        out_shape=jax.ShapeDtypeStruct(queries.shape, bf16),
        in_specs=[pl.BlockSpec(memory_space=pltpu.SMEM)] + [anywhere] * 5,
        out_specs=anywhere,
        scratch_shapes=[
            pltpu.VMEM((members, CORES, 2, parts[s % len(parts)], HEAD_SIZE), bf16)
            for s in range(stages)
        ] + [
            pltpu.VMEM((CHUNKS, CORES, 2, BLK, HEAD_SIZE), bf16),
            pltpu.VMEM((stages, set_size, TOPK, 2, max(parts), HEAD_SIZE), bf16),
            pltpu.VMEM((stages, TOPK, 2, max(parts) * holders, HEAD_SIZE), bf16),
            pltpu.VMEM((CHUNKS, 2, BLK, HEAD_SIZE), bf16),
            pltpu.VMEM((CHUNKS, BLK, WIDE), bf16),
            pltpu.VMEM((CHUNKS, BLK, WIDE), bf16),
            pltpu.VMEM((SHARE, BLK, 2 * HEAD_SIZE), jnp.float32),
            pltpu.VMEM((SHARE, BLK, HEAD_SIZE), jnp.float32),
            dma((CHUNKS,)), dma((stages,)), dma((stages,)), dma((stages, 2)), dma((stages,)),
            dma((stages,)), dma((stages,)),
            dma, dma((CHUNKS,)), dma, dma((CHUNKS,)), dma, dma, dma,
        ],
        compiler_params=pltpu.CompilerParams(
            collective_id=0, has_side_effects=True, vmem_limit_bytes=56 * 1024 * 1024
        ),
        cost_estimate=pl.CostEstimate(
            flops=4 * half * QUERY_HEADS * HEAD_SIZE * (TOPK + 1) * BLK,
            bytes_accessed=16 << 20,
            transcendentals=half * QUERY_HEADS * (TOPK + 1) * BLK,
        ),
    )(selected.T, queries, stretch_keys, stretch_values, cache_keys, cache_values)


def solution(mesh):
    split = P(("groups", "seq"), None)
    return jax.shard_map(
        per_device,
        mesh=mesh,
        in_specs=(split, split, split, split, split, P("groups", None)),
        out_specs=split,
        check_vma=False,
    )
```

```python
import functools

import jax
import jax.numpy as jnp
from jax import lax
from jax.experimental import pallas as pl
from jax.experimental.pallas import tpu as pltpu
from jax.sharding import PartitionSpec as P

QUERY_HEADS = 32
KEY_VALUE_HEADS = 8
HEAD_SIZE = 128
BLK = 512
TOPK = 3
CORES = 2
CHUNKS = KEY_VALUE_HEADS // CORES
SHARE = QUERY_HEADS // KEY_VALUE_HEADS
WIDE = SHARE * HEAD_SIZE
SCALE = HEAD_SIZE ** (-0.5) * 1.4426950408889634
MESH = pl.DeviceIdType.MESH


CONTRACT = (((1,), (1,)), ((), ()))


def weighted(scores, largest, values):
    weights = jnp.exp2(scores * SCALE - largest * SCALE).astype(jnp.bfloat16)
    both = jnp.concatenate([values, jnp.ones_like(values)], axis=1)
    return jnp.dot(weights, both, preferred_element_type=jnp.float32)


def product(q, keys):
    return lax.dot_general(q, keys, CONTRACT, preferred_element_type=jnp.float32)


def attend_first(q, keys, values, own_keys, own_values, first_row):
    scores, own = product(q, keys), product(q, own_keys)
    row = lax.broadcasted_iota(jnp.int32, own.shape, 0) + first_row
    column = lax.broadcasted_iota(jnp.int32, own.shape, 1)
    own = jnp.where(column <= row, own, -1e30)
    largest = jnp.maximum(
        jnp.max(scores, axis=-1, keepdims=True), jnp.max(own, axis=-1, keepdims=True)
    )
    return weighted(scores, largest, values) + weighted(own, largest, own_values), largest


def attend_later(q, keys, values, both, before):
    scores = product(q, keys)
    largest = jnp.maximum(before, jnp.max(scores, axis=-1, keepdims=True))
    both = both * jnp.exp2((before - largest) * SCALE) + weighted(scores, largest, values)
    return both, largest


def kernel(
    members, holders, relayed, parts,
    selected, queries, stretch_keys, stretch_values, cache_keys, cache_values,
    out,
    *scratch,
):
    stages = CHUNKS * len(parts)
    held = scratch[:stages]
    staged, packed, kv, own, qs, outs, sums, tops = scratch[stages:stages + 8]
    (stage_sem, spread_send, spread_recv, near_recv, relay_send, fetch_send, fetch_recv,
     own_send, own_recv, q_send, q_recv, o_send, o_recv, o_local) = scratch[stages + 8:]

    me = lax.axis_index("seq")
    core = lax.rem(me, CORES)
    sibling = me + 1 - 2 * core
    mine = lax.rem(me, holders)
    if relayed:
        plane = me // holders
        upper = plane // 2
        set_size = 2 * holders
        base = upper * set_size
        inner = (1 + upper) * holders
        outer = 3 * upper * holders
        facing = (2 - upper) * holders
        away = lax.rem(plane + upper + 1, 2)
    else:
        set_size = holders
        base = (me // holders) * holders
    half = queries.shape[0]
    my_rows = pl.ds(pl.multiple_of(core * half, half), half)
    other_rows = pl.ds(pl.multiple_of((1 - core) * half, half), half)

    for h in range(CHUNKS):
        for c in range(CORES):
            lanes = pl.ds((c * CHUNKS + h) * HEAD_SIZE, HEAD_SIZE)
            for n, source in enumerate((cache_keys, cache_values)):
                pltpu.make_async_copy(
                    source.at[:, lanes], staged.at[h, c, n], stage_sem.at[h]
                ).start()

    barrier = pltpu.get_barrier_semaphore()

    @pl.loop(1, members)
    def _(k):
        pl.semaphore_signal(
            barrier, inc=1, device_id={"seq": lax.rem(me + k, members)}, device_id_type=MESH
        )

    pl.semaphore_wait(barrier, members - 1)

    def rows_of(s, holder):
        n = s % len(parts)
        first = sum(parts[:n]) * holders + holder * parts[n]
        return pl.ds(pl.multiple_of(first, 16), parts[n])

    def spread_near(s):
        h = s // len(parts)

        @pl.loop(0, holders)
        def _(k):
            q = lax.rem(mine + k, holders)
            source = staged.at[h, :, :, rows_of(s, q), :]

            @pl.when(inner + q == me)
            def _():
                pltpu.make_async_copy(source, held[s].at[me], near_recv.at[s, away]).start()

            @pl.when(inner + q != me)
            def _():
                pltpu.make_async_remote_copy(
                    src_ref=source, dst_ref=held[s].at[me],
                    send_sem=spread_send.at[s], recv_sem=near_recv.at[s, away],
                    device_id={"seq": inner + q}, device_id_type=MESH,
                ).start()

    def relay(s):
        for n, first in enumerate((inner, outer)):
            blocks = held[s].at[pl.ds(first, holders)]
            pltpu.make_async_copy(blocks, blocks, near_recv.at[s, n]).wait()
            pltpu.make_async_remote_copy(
                src_ref=blocks, dst_ref=blocks,
                send_sem=relay_send.at[s], recv_sem=spread_recv.at[s],
                device_id={"seq": facing + mine}, device_id_type=MESH,
            ).start()

    def spread(s):
        h = s // len(parts)
        if s % len(parts) == 0:
            pltpu.make_async_copy(staged.at[h], staged.at[h], stage_sem.at[h]).wait()
        if relayed:
            spread_near(s)
            return
        pltpu.make_async_copy(
            staged.at[h, :, :, rows_of(s, mine), :], held[s].at[me], spread_recv.at[s]
        ).start()

        @pl.loop(1, members)
        def _(k):
            to = lax.rem(me + k, members)
            pltpu.make_async_remote_copy(
                src_ref=staged.at[h, :, :, rows_of(s, lax.rem(to, holders)), :],
                dst_ref=held[s].at[me],
                send_sem=spread_send.at[s],
                recv_sem=spread_recv.at[s],
                device_id={"seq": to},
                device_id_type=MESH,
            ).start()

    spread(0)

    def holding(body, s):
        if relayed:
            pl.when(away == 0)(functools.partial(body, s))
        else:
            body(s)


    if relayed:
        spread(1)
        for s in range(2):
            holding(relay, s)
    for h in range(CHUNKS):
        for here in (True, False):
            c = core if here else 1 - core
            q_lanes = pl.ds(pl.multiple_of((c * CHUNKS + h) * WIDE, WIDE), WIDE)
            kv_lanes = pl.ds(pl.multiple_of((c * CHUNKS + h) * HEAD_SIZE, HEAD_SIZE), HEAD_SIZE)
            for source, target, send, recv in (
                (queries.at[:, q_lanes], qs.at[h, my_rows, :], q_send, q_recv),
                (stretch_keys.at[:, kv_lanes], own.at[h, 0, my_rows, :], own_send, own_recv),
                (stretch_values.at[:, kv_lanes], own.at[h, 1, my_rows, :], own_send, own_recv),
            ):
                if here:
                    pltpu.make_async_copy(source, target, recv.at[h]).start()
                else:
                    pltpu.make_async_remote_copy(
                        src_ref=source, dst_ref=target, send_sem=send, recv_sem=recv.at[h],
                        device_id={"seq": sibling}, device_id_type=MESH,
                    ).start()

    for s in range(2 if relayed else 1, stages if not relayed else 3):
        spread(s)

    def fetch(s):
        arrived = held[s].at[pl.ds(0, set_size)] if relayed else held[s]
        pltpu.make_async_copy(arrived, arrived, spread_recv.at[s]).wait()
        piece = parts[s % len(parts)]
        land = kv.at[s, :, :, pl.ds(pl.multiple_of(mine * piece, piece), piece), :]
        kept = pl.ds(0, piece)

        here = me - base

        @pl.loop(0, set_size)
        def _(k):
            i = lax.rem(here + k, set_size)
            to = base + i
            for t in range(TOPK):
                block = selected[t, to // CORES]
                packed[s, i, t, :, 0:piece] = held[s][block, lax.rem(to, CORES)]

            @pl.when(k == 0)
            def _():
                pltpu.make_async_copy(packed.at[s, i, :, :, kept], land, fetch_recv.at[s]).start()

            @pl.when(k > 0)
            def _():
                pltpu.make_async_remote_copy(
                    src_ref=packed.at[s, i, :, :, kept], dst_ref=land,
                    send_sem=fetch_send.at[s], recv_sem=fetch_recv.at[s],
                    device_id={"seq": to}, device_id_type=MESH,
                ).start()

    def picked(s, n, n_part):
        rows = parts[n_part] * holders
        return kv[s, :, n, 0:rows].reshape(TOPK * rows, HEAD_SIZE)

    def await_picked(s, n_part):
        arrived = kv.at[s, :, :, pl.ds(0, parts[n_part] * holders)]
        pltpu.make_async_copy(arrived, arrived, fetch_recv.at[s]).wait()

    def tiles(body):
        @pl.loop(0, SHARE // 2)
        def _(pair):
            for u in range(2):
                g = pair * 2 + u
                lanes = pl.ds(pl.multiple_of(g * HEAD_SIZE, HEAD_SIZE), HEAD_SIZE)
                for r in range(CORES):
                    body(g, lanes, r, pl.ds(r * half, half))

    def first_part(h):
        s = len(parts) * h
        await_picked(s, 0)
        pltpu.make_async_copy(own.at[h], own.at[h], own_recv.at[h]).wait()
        pltpu.make_async_copy(qs.at[h], qs.at[h], q_recv.at[h]).wait()

        def body(g, lanes, r, rows):
            seen = (r + 1) * half
            both, largest = attend_first(
                qs[h, rows, lanes], picked(s, 0, 0), picked(s, 1, 0),
                own[h, 0, 0:seen], own[h, 1, 0:seen], r * half,
            )
            sums[g, rows] = both
            tops[g, rows] = jnp.broadcast_to(largest, (half, HEAD_SIZE))

        tiles(body)

    def later_part(h, n_part):
        s = len(parts) * h + n_part
        await_picked(s, n_part)

        def body(g, lanes, r, rows):
            both, largest = attend_later(
                qs[h, rows, lanes], picked(s, 0, n_part), picked(s, 1, n_part),
                sums[g, rows], tops[g, rows][:, :1],
            )
            if n_part < len(parts) - 1:
                sums[g, rows] = both
                tops[g, rows] = jnp.broadcast_to(largest, (half, HEAD_SIZE))
            else:
                done = both[:, :HEAD_SIZE] / both[:, HEAD_SIZE:]
                outs[h, rows, lanes] = done.astype(jnp.bfloat16)

        tiles(body)
        if n_part == len(parts) - 1:
            give_back(h)

    def give_back(h):
        lanes = pl.ds(pl.multiple_of((core * CHUNKS + h) * WIDE, WIDE), WIDE)
        pltpu.make_async_copy(outs.at[h, my_rows, :], out.at[:, lanes], o_local).start()
        pltpu.make_async_remote_copy(
            src_ref=outs.at[h, other_rows, :], dst_ref=out.at[:, lanes],
            send_sem=o_send, recv_sem=o_recv,
            device_id={"seq": sibling}, device_id_type=MESH,
        ).start()

    @pl.loop(0, stages + 1)
    def _(step):
        for s in range(stages):
            @pl.when(step == s)
            def _():
                if relayed and s + 2 < stages:
                    holding(relay, s + 2)
                if relayed and s + 3 < stages:
                    spread(s + 3)
                holding(fetch, s)

        before = step - 1

        @pl.when((step > 0) & (lax.rem(before, len(parts)) == 0))
        def _():
            first_part(before // len(parts))

        for n_part in range(1, len(parts)):
            @pl.when((step > 0) & (lax.rem(before, len(parts)) == n_part))
            def _():
                later_part(before // len(parts), n_part)

    def await_sent(count, s):
        sent = held[s].at[pl.ds(0, count)]
        pltpu.make_async_copy(sent, sent, spread_send.at[s]).wait()

    def await_held_sent(s):
        if relayed:
            await_sent(holders - 1, s)
            sent = held[s].at[pl.ds(0, set_size)]
            pltpu.make_async_copy(sent, sent, relay_send.at[s]).wait()
        sent = packed.at[s, pl.ds(0, set_size - 1), :, :, pl.ds(0, parts[s % len(parts)])]
        pltpu.make_async_copy(sent, sent, fetch_send.at[s]).wait()

    for s in range(stages):
        if relayed:
            pl.when(away == 1)(functools.partial(await_sent, holders, s))
        else:
            await_sent(members - 1, s)
        holding(await_held_sent, s)
    sent = qs.at[pl.ds(0, CHUNKS // 2)]
    pltpu.make_async_copy(sent, sent, q_send).wait()
    sent = own.at[pl.ds(0, CHUNKS // 2)]
    pltpu.make_async_copy(sent, sent, own_send).wait()
    wide = CHUNKS * WIDE
    kept = out.at[:, pl.ds(pl.multiple_of(core * wide, wide), wide)]
    given = out.at[:, pl.ds(pl.multiple_of((1 - core) * wide, wide), wide)]
    pltpu.make_async_copy(kept, kept, o_local).wait()
    pltpu.make_async_copy(kept, kept, o_send).wait()
    pltpu.make_async_copy(given, given, o_recv).wait()


def per_device(queries, stretch_keys, stretch_values, cache_keys, cache_values, selected):
    members = lax.axis_size("seq")
    half = queries.shape[0]
    assert half * CORES == BLK and cache_keys.shape[0] == BLK
    relayed = members == 16
    holders = members // 4 if relayed else min(members // 2, BLK // 32)
    set_size = 2 * holders if relayed else holders
    parts = (BLK // 16,) * 4 if relayed else (BLK // (2 * holders),) * 2
    stages = CHUNKS * len(parts)
    bf16 = jnp.bfloat16
    dma = pltpu.SemaphoreType.DMA
    anywhere = pl.BlockSpec(memory_space=pl.ANY)
    return pl.pallas_call(
        functools.partial(kernel, members, holders, relayed, parts),
        out_shape=jax.ShapeDtypeStruct(queries.shape, bf16),
        in_specs=[pl.BlockSpec(memory_space=pltpu.SMEM)] + [anywhere] * 5,
        out_specs=anywhere,
        scratch_shapes=[
            pltpu.VMEM((members, CORES, 2, parts[s % len(parts)], HEAD_SIZE), bf16)
            for s in range(stages)
        ] + [
            pltpu.VMEM((CHUNKS, CORES, 2, BLK, HEAD_SIZE), bf16),
            pltpu.VMEM((stages, set_size, TOPK, 2, max(parts), HEAD_SIZE), bf16),
            pltpu.VMEM((stages, TOPK, 2, max(parts) * holders, HEAD_SIZE), bf16),
            pltpu.VMEM((CHUNKS, 2, BLK, HEAD_SIZE), bf16),
            pltpu.VMEM((CHUNKS, BLK, WIDE), bf16),
            pltpu.VMEM((CHUNKS, BLK, WIDE), bf16),
            pltpu.VMEM((SHARE, BLK, 2 * HEAD_SIZE), jnp.float32),
            pltpu.VMEM((SHARE, BLK, HEAD_SIZE), jnp.float32),
            dma((CHUNKS,)), dma((stages,)), dma((stages,)), dma((stages, 2)), dma((stages,)),
            dma((stages,)), dma((stages,)),
            dma, dma((CHUNKS,)), dma, dma((CHUNKS,)), dma, dma, dma,
        ],
        compiler_params=pltpu.CompilerParams(
            collective_id=0, has_side_effects=True, vmem_limit_bytes=56 * 1024 * 1024
        ),
        cost_estimate=pl.CostEstimate(
            flops=4 * half * QUERY_HEADS * HEAD_SIZE * (TOPK + 1) * BLK,
            bytes_accessed=16 << 20,
            transcendentals=half * QUERY_HEADS * (TOPK + 1) * BLK,
        ),
    )(selected.T, queries, stretch_keys, stretch_values, cache_keys, cache_values)


def solution(mesh):
    split = P(("groups", "seq"), None)
    return jax.shard_map(
        per_device,
        mesh=mesh,
        in_specs=(split, split, split, split, split, P("groups", None)),
        out_specs=split,
        check_vma=False,
    )
```
